32 devices in a mesh: grp: 2 (over y), dp: 4 (over z), mod: 4 (over x, core).
Axes of the slice: x: 2, y: 2, z: 4, core: 2. Of those that a mesh axis runs over, the one named last changes fastest.
Arguments:
- queries: bfloat16 [32, 16, 4096], P('dp', 'mod'), may hold values from -0.119628906 to 0.119628906
- batch: int32 [32], P('dp'), may hold values from 0 to 1
- inv_out: float32 [2, 16, 64, 64], P(None, 'mod'), as said below
- inv_in: float32 [2, 16, 64, 64], P(None, 'mod'), as said below
- train_store: bfloat16 [1024, 16, 4096], P(('grp', 'dp'), 'mod'), parts along dimension 0, may hold values from -6 to 6
- row_scale: float32 [1024, 16], P(('grp', 'dp'), 'mod'), parts along dimension 0, may hold values from 0.2 to 2
Outputs:
- scores: float32 [32, 1024], P('mod', ('grp', 'dp')), parts along dimension 1
The draws below stay inside these ranges and needn't reach their ends.
There are 2 independent parts, one for each index of `grp`. The reference program is written for one: setup_inputs(seed, part) draws one part's arguments, and reference() takes and returns one part's arrays. A program takes and returns all parts, laid end to end along the dimension named above; an argument that names none is the same for every part. Nothing has to cross between parts.
Inputs may be any that keep to these rules, and one draw needn't show every extreme that they name: `inv_out`: symmetric, each matrix of the form diagonal plus a smaller symmetric part. `inv_in`: symmetric, each matrix of the form diagonal plus a smaller symmetric part.
All inputs are finite; a program needn't handle non-finite values.
Results may differ from the reference program's by a relative error of at most 0.0029.
Values may be sent and summed in bfloat16 or wider, within the bound.
A program may use at most 64 MiB of HBM per device.

```python
import math
import jax
import jax.numpy as jnp
from jax import lax

Q = 32
KOUT = 64
KIN = 64
MODULES = 16
TRAIN = 512


def symmetric_inverse(key, width):
    first, second = jax.random.split(key)
    diag = jnp.exp(jax.random.uniform(first, (2, MODULES, width), jnp.float32, math.log(0.6), math.log(2.0)))
    noise = jax.random.normal(second, (2, MODULES, width, width), jnp.float32)
    sym_part = (noise + jnp.swapaxes(noise, 2, 3)) * (0.25 / math.sqrt(2.0 * width))
    eye = jnp.eye(width, dtype=jnp.float32)
    return sym_part * (1.0 - eye) + eye * diag[:, :, :, None]


def draw_inv_out(key, part):
    key = jax.random.fold_in(key, 11)
    return symmetric_inverse(key, KOUT)


def draw_inv_in(key, part):
    key = jax.random.fold_in(key, 23)
    return symmetric_inverse(key, KIN)


def place_ends(drawn, own_key, least, high):
    shape = drawn.shape
    index_at = [jax.random.randint(jax.random.fold_in(own_key, axis), (), 0, shape[axis]) for axis in range(len(shape))]
    drawn = drawn.at[tuple(index_at)].set(least)
    longest = shape.index(max(shape))
    index_at[longest] = (index_at[longest] + 1) % shape[longest]
    return drawn.at[tuple(index_at)].set(high)


def strengthened(values, own_key, source, target, blocks, factor):
    def block_of(axis_at):
        return (jnp.arange(values.shape[axis_at]) // (values.shape[axis_at] // blocks)).reshape((-1,) + (1,) * (values.ndim - 1 - axis_at))

    first = jax.random.permutation(own_key, blocks)[block_of(target)]
    second = (block_of(target) + blocks // 2) % blocks
    return jnp.where((block_of(source) == first) | (block_of(source) == second), factor * values, values)


def steps_of(own_key, shape, cuts, smallest, top_value):
    level = 1.0
    for position, shards_of in cuts:
        heights = jax.random.uniform(jax.random.fold_in(jax.random.fold_in(own_key, 6), position), (shards_of,), jnp.float32, smallest / len(cuts), top_value / len(cuts))
        level = level * jnp.repeat(jnp.exp(heights), shape[position] // shards_of).reshape((-1,) + (1,) * (len(shape) - 1 - position))
    return level


def scatter_about(rng, dims, deviation, limit, cuts=(), kind=jnp.bfloat16):
    values = deviation * jax.random.normal(rng, dims, jnp.float32)
    if cuts:
        values = values * steps_of(rng, dims, cuts, -0.22, 0.18)
    return jnp.clip(values, -limit, limit).astype(kind)


def bell_draw_with(key, extent, scale, bound, cuts, heavy, kind=jnp.bfloat16):
    drawn = scale * jax.random.normal(key, extent, jnp.float32)
    if cuts:
        drawn = drawn * steps_of(key, extent, cuts, -0.22, 0.18)
    return jnp.clip(strengthened(drawn, jax.random.fold_in(key, 3), *heavy), -bound, bound).astype(kind)


def setup_inputs(seed: int = 0, part: int = 0) -> dict:
    streams_of = jax.random.split(jax.random.key(seed), 7)
    part_splits = jax.random.split(jax.random.fold_in(streams_of[6], part), 7)
    return {
        "queries": bell_draw_with(streams_of[0], (Q, MODULES, KOUT * KIN), 0.02, 0.119628906, ((0, 4), (1, 4)), (1, 0, 4, 2.0)),
        "batch": place_ends(jax.random.randint(streams_of[1], (Q,), 0, 2), jax.random.fold_in(streams_of[1], 1), 0, 1).astype(jnp.int32),
        "inv_out": draw_inv_out(jax.random.fold_in(streams_of[6], 71), part),
        "inv_in": draw_inv_in(jax.random.fold_in(streams_of[6], 71), part),
        "train_store": scatter_about(part_splits[4], (TRAIN, MODULES, KOUT * KIN), 1.0, 6.0, ((0, 4), (1, 4))),
        "row_scale": jnp.clip(jnp.exp(math.log(2.0) - 2.3025851 * jax.random.uniform(part_splits[5], (TRAIN, MODULES), jnp.float32) ** steps_of(part_splits[5], (TRAIN, MODULES), ((0, 4), (1, 4)), -0.2, 0.2)), 0.2, 2.0),
    }


def reference(queries, batch, inv_out, inv_in, train_store, row_scale):
    grad = queries.astype(jnp.float32).reshape(Q, MODULES, KOUT, KIN)
    left = jnp.einsum("qmij,qmjk->qmik", inv_out[batch], grad, precision=lax.Precision.HIGHEST)
    both = jnp.einsum("qmik,qmkl->qmil", left, inv_in[batch], precision=lax.Precision.HIGHEST)
    pre = both.reshape(Q, MODULES, KOUT * KIN).astype(jnp.bfloat16)

    def step(total, index):
        slab = lax.dynamic_index_in_dim(train_store, index, 1, keepdims=False)
        rows = lax.dynamic_index_in_dim(pre, index, 1, keepdims=False)
        weight = lax.dynamic_index_in_dim(row_scale, index, 1, keepdims=False)
        raw = jnp.dot(rows, slab.T, preferred_element_type=jnp.float32)
        return total + raw * weight[None, :], None

    start = jnp.zeros((Q, TRAIN), jnp.float32)
    scores, unused = lax.scan(step, start, jnp.arange(MODULES, dtype=jnp.int32))
    return scores
```

```python
import functools

import jax
import jax.numpy as jnp
from jax import lax
from jax.experimental import pallas as pl
from jax.experimental.pallas import tpu as pltpu
from jax.sharding import PartitionSpec as P

F32 = jnp.float32
BF16 = jnp.bfloat16
MESH = pl.DeviceIdType.MESH
LANES = 128


def pieces(values):
    high = values.astype(BF16)
    low = (values - high.astype(F32)).astype(BF16)
    return high, low


def mat(a, b):
    return jnp.dot(a, b, preferred_element_type=F32)


def mat_t(a, b):
    return lax.dot_general(a, b, (((1,), (1,)), ((), ())), preferred_element_type=F32)


def iota(shape, dim):
    return lax.broadcasted_iota(jnp.int32, shape, dim)


def ones_where(cond):
    return jnp.where(cond, 1.0, 0.0).astype(BF16)


def three(values):
    high = values.astype(BF16)
    rest = values - high.astype(F32)
    mid = rest.astype(BF16)
    low = (rest - mid.astype(F32)).astype(BF16)
    return high, mid, low


def kernel(sizes, q_ref, batch_ref, out_ref_in, in_ref_in, train_ref, scale_ref, res_ref,
           tcat, preb, right, left, scale_x, part, got,
           t_sem, z_send, z_recv, y_send, y_recv, m_send, m_recv):
    dp, nmod, own_q, mods, width, tiles, rows_t = sizes
    half_q = own_q // 2
    group = 16
    kts = group // mods
    cuts = tiles // kts
    rows = tiles * mods
    cols = own_q * group
    y, z, md = lax.axis_index("grp"), lax.axis_index("dp"), lax.axis_index("mod")
    other = 1 - y

    barrier = pltpu.get_barrier_semaphore()
    pl.semaphore_signal(barrier, inc=1, device_id={"grp": other}, device_id_type=MESH)
    for s in range(1, dp):
        pl.semaphore_signal(barrier, inc=1, device_id={"dp": lax.rem(z + s, dp)}, device_id_type=MESH)
    for s in range(1, nmod):
        pl.semaphore_signal(barrier, inc=1, device_id={"mod": lax.rem(md + s, nmod)}, device_id_type=MESH)

    def train_copy(g):
        return pltpu.make_async_copy(
            train_ref.at[:, pl.ds(group * g, group), :],
            tcat.at[:, :, pl.ds(LANES * g, LANES)],
            t_sem.at[g],
        )

    for g in range(cuts):
        train_copy(g).start()

    spread = ones_where(iota((width, 4 * width), 0) == iota((width, 4 * width), 1) % width)
    shape4 = (mods, 2, width, 4 * width)
    block = iota(shape4, 3) // width
    keep_r = (block % 2) == ((block // 2) ^ iota(shape4, 1))
    line = iota((2 * rows, mods * width), 0)
    line_half, line_in = line // rows, line % rows
    src = iota((2 * rows, mods * width), 1)
    pick_rows = ones_where((src // width == line_in % mods) & (src % width == 2 * (line_in // mods) + line_half))
    lcol = iota((width, 2 * rows), 1)
    col_half, col_in = lcol // rows, lcol % rows
    pick_cols = [
        ones_where(iota((width, 2 * rows), 0) == 2 * (col_in // mods) + (col_half ^ h)) for h in range(2)
    ]
    keep_l = iota((rows, 2 * rows), 0) % mods == iota((rows, 2 * rows), 1) % mods
    for b in range(2):
        for i, piece in enumerate(pieces(in_ref_in[b].reshape(mods * width, width))):
            wide = mat(piece, spread).reshape(mods, 1, width, 4 * width)
            wide = jnp.where(keep_r, jnp.broadcast_to(wide, shape4), 0.0)
            right[b, i] = wide.reshape(mods * 2 * width, 4 * width).astype(BF16)
        for i, piece in enumerate(pieces(out_ref_in[b].reshape(mods * width, width))):
            lines = mat(pick_rows, piece).astype(BF16)
            for h in range(2):
                full = mat(lines[h * rows:(h + 1) * rows], pick_cols[h])
                left[b, i, h * rows:(h + 1) * rows] = jnp.where(keep_l, full, 0.0).astype(BF16)

    def precondition(q, slot, at):
        b = batch_ref[q]
        x = q_ref[q]
        row_mod = iota((rows, LANES), 0) % mods
        zero = jnp.zeros_like(x)
        wide = jnp.concatenate([jnp.where(row_mod == m, x, zero) for m in range(mods)], axis=1)
        pair = mat(wide, right[b, 0]) + mat(wide, right[b, 1])
        stacked = jnp.concatenate([pair[:, :LANES], pair[:, LANES:]], axis=0)
        high, low = pieces(stacked)
        both = mat(left[b, 0], high) + (mat(left[b, 0], low) + mat(left[b, 1], high))
        lane = iota((rows, LANES), 1)
        pre = jnp.where(lane < width, both[:rows], both[rows:]).astype(BF16)
        for g in range(cuts):
            preb[z, slot, at, :, g * LANES:(g + 1) * LANES] = pre[g * group:(g + 1) * group]

    for i in range(half_q):
        precondition(y * half_q + i, y, i)

    def z_copy(origin, target):
        return pltpu.make_async_remote_copy(
            src_ref=preb.at[origin, y], dst_ref=preb.at[origin, y],
            send_sem=z_send.at[target], recv_sem=z_recv.at[origin],
            device_id={"dp": target}, device_id_type=MESH)

    def y_copy(origin, part_at):
        return pltpu.make_async_remote_copy(
            src_ref=preb.at[origin, part_at], dst_ref=preb.at[origin, part_at],
            send_sem=y_send.at[origin], recv_sem=y_recv.at[origin],
            device_id={"grp": other}, device_id_type=MESH)

    def m_copy(to, frm):
        return pltpu.make_async_remote_copy(
            src_ref=part.at[to], dst_ref=got.at[frm],
            send_sem=m_send.at[to], recv_sem=m_recv.at[frm],
            device_id={"mod": to}, device_id_type=MESH)

    pl.semaphore_wait(barrier, dp + nmod - 1)
    for s in range(1, dp):
        z_copy(z, lax.rem(z + s, dp)).start()

    for i in range(half_q):
        precondition(other * half_q + i, other, i)

    pick_mod = ones_where(iota((mods, cols), 0) == iota((mods, cols), 1) % mods)
    scale_x[...] = sum(
        lax.dot_general(p, pick_mod, (((0,), (0,)), ((), ())), preferred_element_type=F32)
        for p in three(scale_ref[...]))
    fold = ones_where(iota((own_q, cols), 1) // group == iota((own_q, cols), 0))

    for g in range(cuts):
        train_copy(g).wait()

    def score(origin):
        pre = preb[origin].reshape(cols, cuts * LANES)
        raw = mat_t(tcat[...].reshape(rows_t * group, cuts * LANES), pre).reshape(rows_t, group, cols)
        keep = iota((rows_t, group, cols), 1) == iota((rows_t, group, cols), 2) % group
        picked = jnp.sum(jnp.where(keep, raw, 0.0), axis=1) * scale_x[...]
        part[origin] = sum(mat_t(fold, p) for p in three(picked))

        @pl.when(origin != md)
        def _():
            m_copy(origin, md).start()

    score(z)

    for s in range(1, dp):
        origin = lax.rem(z + dp - s, dp)
        z_copy(origin, origin).wait_recv()
        y_copy(origin, y).start()

    def step(s, carry):
        origin = lax.rem(z + dp - s, dp)
        y_copy(origin, other).wait_recv()
        score(origin)
        return carry

    lax.fori_loop(1, dp, step, 0)

    total = part[md]
    for s in range(1, nmod):
        frm = lax.rem(md + s, nmod)
        m_copy(md, frm).wait_recv()
        total = total + got[frm]
    res_ref[...] = total

    for s in range(1, dp):
        at = lax.rem(z + s, dp)
        z_copy(z, at).wait_send()
        y_copy(at, y).wait_send()
    for s in range(1, nmod):
        m_copy(lax.rem(md + s, nmod), md).wait_send()


def shards(queries, batch, inv_out, inv_in, train_store, row_scale):
    own_q, mods, flat = queries.shape
    width = inv_in.shape[-1]
    rows_t = train_store.shape[0]
    dp, nmod = lax.axis_size("dp"), lax.axis_size("mod")
    tiles = flat // LANES
    rows = tiles * mods

    def by_tile(a):
        return jnp.transpose(a.reshape(-1, mods, tiles, LANES), (0, 2, 1, 3)).reshape(-1, rows, LANES)

    sizes = (dp, nmod, own_q, mods, width, tiles, rows_t)
    vmem = pl.BlockSpec(memory_space=pltpu.VMEM)
    cuts = rows // 16
    return pl.pallas_call(
        functools.partial(kernel, sizes),
        out_shape=jax.ShapeDtypeStruct((own_q, rows_t), F32),
        in_specs=[vmem, pl.BlockSpec(memory_space=pltpu.SMEM), vmem, vmem,
                  pl.BlockSpec(memory_space=pl.ANY), vmem],
        out_specs=vmem,
        scratch_shapes=[
            pltpu.VMEM((rows_t, 16, cuts * LANES), BF16),
            pltpu.VMEM((dp, 2, own_q // 2, 16, cuts * LANES), BF16),
            pltpu.VMEM((2, 2, mods * 2 * width, 4 * width), BF16),
            pltpu.VMEM((2, 2, 2 * rows, 2 * rows), BF16),
            pltpu.VMEM((rows_t, own_q * 16), F32),
            pltpu.VMEM((nmod, own_q, rows_t), F32),
            pltpu.VMEM((nmod, own_q, rows_t), F32),
            pltpu.SemaphoreType.DMA((cuts,)),
            pltpu.SemaphoreType.DMA((dp,)),
            pltpu.SemaphoreType.DMA((dp,)),
            pltpu.SemaphoreType.DMA((dp,)),
            pltpu.SemaphoreType.DMA((dp,)),
            pltpu.SemaphoreType.DMA((nmod,)),
            pltpu.SemaphoreType.DMA((nmod,)),
        ],
        compiler_params=pltpu.CompilerParams(
            collective_id=0, has_side_effects=True, vmem_limit_bytes=40 * 1024 * 1024),
    )(by_tile(queries), batch, inv_out, inv_in, by_tile(train_store), jnp.transpose(row_scale))


def solution(mesh):
    in_specs = (
        P("dp", "mod", None),
        P("dp"),
        P(None, "mod", None, None),
        P(None, "mod", None, None),
        P(("grp", "dp"), "mod", None),
        P(("grp", "dp"), "mod"),
    )
    out_specs = P("mod", ("grp", "dp"))
    return jax.shard_map(shards, mesh=mesh, in_specs=in_specs, out_specs=out_specs, check_vma=False)
```

```python
import functools

import jax
import jax.numpy as jnp
from jax import lax
from jax.experimental import pallas as pl
from jax.experimental.pallas import tpu as pltpu
from jax.sharding import PartitionSpec as P

F32 = jnp.float32
BF16 = jnp.bfloat16
MESH = pl.DeviceIdType.MESH
LANES = 128


def pieces(values):
    high = values.astype(BF16)
    low = (values - high.astype(F32)).astype(BF16)
    return high, low


def mat(a, b):
    return jnp.dot(a, b, preferred_element_type=F32)


def mat_t(a, b):
    return lax.dot_general(a, b, (((1,), (1,)), ((), ())), preferred_element_type=F32)


def iota(shape, dim):
    return lax.broadcasted_iota(jnp.int32, shape, dim)


def ones_where(cond):
    return jnp.where(cond, 1.0, 0.0).astype(BF16)


def three(values):
    high = values.astype(BF16)
    rest = values - high.astype(F32)
    mid = rest.astype(BF16)
    low = (rest - mid.astype(F32)).astype(BF16)
    return high, mid, low


def kernel(sizes, q_hbm, batch_ref, out_hbm, in_hbm, train_ref, scale_hbm, res_ref,
           q_ref, out_ref_in, in_ref_in, scale_ref,
           tcat, preb, right, left, scale_x, part, got,
           l_sem, t_sem, z_send, z_recv, y_send, y_recv, m_send, m_recv):
    dp, nmod, own_q, mods, width, tiles, rows_t = sizes
    half_q = own_q // 2
    group = 16
    kts = group // mods
    cuts = tiles // kts
    rows = tiles * mods
    cols = own_q * group
    y, z, md = lax.axis_index("grp"), lax.axis_index("dp"), lax.axis_index("mod")
    other = 1 - y

    locals_in = [
        pltpu.make_async_copy(src, dst, l_sem.at[i])
        for i, (src, dst) in enumerate(
            ((out_hbm, out_ref_in), (in_hbm, in_ref_in), (q_hbm, q_ref), (scale_hbm, scale_ref)))
    ]
    for copy in locals_in:
        copy.start()

    barrier = pltpu.get_barrier_semaphore()
    pl.semaphore_signal(barrier, inc=1, device_id={"grp": other}, device_id_type=MESH)

    @pl.when(z > 0)
    def _():
        pl.semaphore_signal(barrier, inc=1, device_id={"dp": z - 1}, device_id_type=MESH)

    @pl.when(z < dp - 1)
    def _():
        pl.semaphore_signal(barrier, inc=1, device_id={"dp": z + 1}, device_id_type=MESH)

    for s in range(1, nmod):
        pl.semaphore_signal(barrier, inc=1, device_id={"mod": lax.rem(md + s, nmod)}, device_id_type=MESH)

    def train_copy(g):
        return pltpu.make_async_copy(
            train_ref.at[:, pl.ds(group * g, group), :],
            tcat.at[:, :, pl.ds(LANES * g, LANES)],
            t_sem.at[g],
        )

    for g in range(cuts):
        train_copy(g).start()

    spread = ones_where(iota((width, 4 * width), 0) == iota((width, 4 * width), 1) % width)
    shape4 = (mods, 2, width, 4 * width)
    block = iota(shape4, 3) // width
    keep_r = (block % 2) == ((block // 2) ^ iota(shape4, 1))
    line = iota((2 * rows, mods * width), 0)
    line_half, line_in = line // rows, line % rows
    src = iota((2 * rows, mods * width), 1)
    pick_rows = ones_where((src // width == line_in % mods) & (src % width == 2 * (line_in // mods) + line_half))
    lcol = iota((width, 2 * rows), 1)
    col_half, col_in = lcol // rows, lcol % rows
    pick_cols = [
        ones_where(iota((width, 2 * rows), 0) == 2 * (col_in // mods) + (col_half ^ h)) for h in range(2)
    ]
    keep_l = iota((rows, 2 * rows), 0) % mods == iota((rows, 2 * rows), 1) % mods
    locals_in[0].wait()
    locals_in[1].wait()
    for b in range(2):
        for i, piece in enumerate(pieces(in_ref_in[b].reshape(mods * width, width))):
            wide = mat(piece, spread).reshape(mods, 1, width, 4 * width)
            wide = jnp.where(keep_r, jnp.broadcast_to(wide, shape4), 0.0)
            right[b, i] = wide.reshape(mods * 2 * width, 4 * width).astype(BF16)
        for i, piece in enumerate(pieces(out_ref_in[b].reshape(mods * width, width))):
            lines = mat(pick_rows, piece).astype(BF16)
            for h in range(2):
                full = mat(lines[h * rows:(h + 1) * rows], pick_cols[h])
                left[b, i, h * rows:(h + 1) * rows] = jnp.where(keep_l, full, 0.0).astype(BF16)

    def precondition(q, slot, at):
        b = batch_ref[q]
        x = q_ref[q]
        row_mod = iota((rows, LANES), 0) % mods
        zero = jnp.zeros_like(x)
        wide = jnp.concatenate([jnp.where(row_mod == m, x, zero) for m in range(mods)], axis=1)
        pair = mat(wide, right[b, 0]) + mat(wide, right[b, 1])
        stacked = jnp.concatenate([pair[:, :LANES], pair[:, LANES:]], axis=0)
        high, low = pieces(stacked)
        both = mat(left[b, 0], high) + (mat(left[b, 0], low) + mat(left[b, 1], high))
        lane = iota((rows, LANES), 1)
        pre = jnp.where(lane < width, both[:rows], both[rows:]).astype(BF16)
        for g in range(cuts):
            preb[z, slot, at, :, g * LANES:(g + 1) * LANES] = pre[g * group:(g + 1) * group]

    def z_copy(origin, i, way):
        return pltpu.make_async_remote_copy(
            src_ref=preb.at[origin, y, i], dst_ref=preb.at[origin, y, i],
            send_sem=z_send.at[way, origin, i], recv_sem=z_recv.at[origin, i],
            device_id={"dp": z + (1 - 2 * way)}, device_id_type=MESH)

    def y_copy(origin, part_at, i):
        return pltpu.make_async_remote_copy(
            src_ref=preb.at[origin, part_at, i], dst_ref=preb.at[origin, part_at, i],
            send_sem=y_send.at[origin, i], recv_sem=y_recv.at[origin, i],
            device_id={"grp": other}, device_id_type=MESH)

    def m_copy(to, frm):
        return pltpu.make_async_remote_copy(
            src_ref=part.at[to], dst_ref=got.at[frm],
            send_sem=m_send.at[to], recv_sem=m_recv.at[frm],
            device_id={"mod": to}, device_id_type=MESH)

    def has_next(way):
        return z < dp - 1 if way == 0 else z > 0

    locals_in[2].wait()
    for i in range(half_q):
        precondition(y * half_q + i, y, i)
        if i == 0:
            at_end = (z == 0) | (z == dp - 1)

            @pl.when(at_end)
            def _():
                pl.semaphore_wait(barrier, nmod + 1)

            @pl.when(jnp.logical_not(at_end))
            def _():
                pl.semaphore_wait(barrier, nmod + 2)

        for way in range(2):
            @pl.when(has_next(way))
            def _():
                z_copy(z, i, way).start()

    locals_in[3].wait()
    pick_mod = ones_where(iota((mods, cols), 0) == iota((mods, cols), 1) % mods)
    scale_x[...] = sum(
        lax.dot_general(p, pick_mod, (((0,), (0,)), ((), ())), preferred_element_type=F32)
        for p in three(scale_ref[...]))
    fold = ones_where(iota((own_q, cols), 1) // group == iota((own_q, cols), 0))

    for g in range(cuts):
        train_copy(g).wait()

    def score(origin):
        pre = preb[origin].reshape(cols, cuts * LANES)
        raw = mat_t(tcat[...].reshape(rows_t * group, cuts * LANES), pre).reshape(rows_t, group, cols)
        keep = iota((rows_t, group, cols), 1) == iota((rows_t, group, cols), 2) % group
        picked = jnp.sum(jnp.where(keep, raw, 0.0), axis=1) * scale_x[...]
        part[origin] = sum(mat_t(fold, p) for p in three(picked))

        @pl.when(origin != md)
        def _():
            m_copy(origin, md).start()

    def source(d, way):
        origin = z - d if way == 0 else z + d
        return jnp.clip(origin, 0, dp - 1), (origin >= 0) & (origin < dp)

    def pass_on(d, i):
        for way in range(2):
            origin, there = source(d, way)

            @pl.when(there)
            def _():
                z_copy(origin, i, way).wait_recv()

                @pl.when(has_next(way))
                def _():
                    z_copy(origin, i, way).start()

                y_copy(origin, y, i).start()

    def use(d):
        for way in range(2):
            origin, there = source(d, way)

            @pl.when(there)
            def _():
                for i in range(half_q):
                    y_copy(origin, other, i).wait_recv()
                score(origin)

    for i in range(half_q):
        pass_on(1, i)
        precondition(other * half_q + i, other, i)
    score(z)

    def step(d, carry):
        for i in range(half_q):
            pass_on(d, i)
        use(d - 1)
        return carry

    lax.fori_loop(2, dp, step, 0)
    use(dp - 1)

    total = part[md]
    for s in range(1, nmod):
        frm = lax.rem(md + s, nmod)
        m_copy(md, frm).wait_recv()
        total = total + got[frm]
    res_ref[...] = total

    def drain(origin, carry):
        for i in range(half_q):
            @pl.when((origin <= z) & (z < dp - 1))
            def _():
                z_copy(origin, i, 0).wait_send()

            @pl.when((origin >= z) & (z > 0))
            def _():
                z_copy(origin, i, 1).wait_send()

            @pl.when(origin != z)
            def _():
                y_copy(origin, y, i).wait_send()

        return carry

    lax.fori_loop(0, dp, drain, 0)
    for s in range(1, nmod):
        m_copy(lax.rem(md + s, nmod), md).wait_send()


def shards(queries, batch, inv_out, inv_in, train_store, row_scale):
    own_q, mods, flat = queries.shape
    width = inv_in.shape[-1]
    rows_t = train_store.shape[0]
    dp, nmod = lax.axis_size("dp"), lax.axis_size("mod")
    tiles = flat // LANES
    rows = tiles * mods

    def by_tile(a):
        return jnp.transpose(a.reshape(-1, mods, tiles, LANES), (0, 2, 1, 3)).reshape(-1, rows, LANES)

    sizes = (dp, nmod, own_q, mods, width, tiles, rows_t)
    vmem = pl.BlockSpec(memory_space=pltpu.VMEM)
    hbm = pl.BlockSpec(memory_space=pl.ANY)
    half_q = own_q // 2
    cuts = rows // 16
    return pl.pallas_call(
        functools.partial(kernel, sizes),
        out_shape=jax.ShapeDtypeStruct((own_q, rows_t), F32),
        in_specs=[hbm, pl.BlockSpec(memory_space=pltpu.SMEM), hbm, hbm, hbm, hbm],
        out_specs=vmem,
        scratch_shapes=[
            pltpu.VMEM((own_q, rows, LANES), BF16),
            pltpu.VMEM(inv_out.shape, F32),
            pltpu.VMEM(inv_in.shape, F32),
            pltpu.VMEM((mods, rows_t), F32),
            pltpu.VMEM((rows_t, 16, cuts * LANES), BF16),
            pltpu.VMEM((dp, 2, own_q // 2, 16, cuts * LANES), BF16),
            pltpu.VMEM((2, 2, mods * 2 * width, 4 * width), BF16),
            pltpu.VMEM((2, 2, 2 * rows, 2 * rows), BF16),
            pltpu.VMEM((rows_t, own_q * 16), F32),
            pltpu.VMEM((nmod, own_q, rows_t), F32),
            pltpu.VMEM((nmod, own_q, rows_t), F32),
            pltpu.SemaphoreType.DMA((4,)),
            pltpu.SemaphoreType.DMA((cuts,)),
            pltpu.SemaphoreType.DMA((2, dp, half_q)),
            pltpu.SemaphoreType.DMA((dp, half_q)),
            pltpu.SemaphoreType.DMA((dp, half_q)),
            pltpu.SemaphoreType.DMA((dp, half_q)),
            pltpu.SemaphoreType.DMA((nmod,)),
            pltpu.SemaphoreType.DMA((nmod,)),
        ],
        compiler_params=pltpu.CompilerParams(
            collective_id=0, has_side_effects=True, vmem_limit_bytes=60 * 1024 * 1024),
    )(by_tile(queries), batch, inv_out, inv_in, by_tile(train_store), jnp.transpose(row_scale))


def solution(mesh):
    in_specs = (
        P("dp", "mod", None),
        P("dp"),
        P(None, "mod", None, None),
        P(None, "mod", None, None),
        P(("grp", "dp"), "mod", None),
        P(("grp", "dp"), "mod"),
    )
    out_specs = P("mod", ("grp", "dp"))
    return jax.shard_map(shards, mesh=mesh, in_specs=in_specs, out_specs=out_specs, check_vma=False)
```

```python
import functools

import jax
import jax.numpy as jnp
from jax import lax
from jax.experimental import pallas as pl
from jax.experimental.pallas import tpu as pltpu
from jax.sharding import PartitionSpec as P

F32 = jnp.float32
BF16 = jnp.bfloat16
MESH = pl.DeviceIdType.MESH
LANES = 128


def pieces(values):
    high = values.astype(BF16)
    low = (values - high.astype(F32)).astype(BF16)
    return high, low


def mat(a, b):
    return jnp.dot(a, b, preferred_element_type=F32)


def mat_t(a, b):
    return lax.dot_general(a, b, (((1,), (1,)), ((), ())), preferred_element_type=F32)


def iota(shape, dim):
    return lax.broadcasted_iota(jnp.int32, shape, dim)


def ones_where(cond):
    return jnp.where(cond, 1.0, 0.0).astype(BF16)


def three(values):
    high = values.astype(BF16)
    rest = values - high.astype(F32)
    mid = rest.astype(BF16)
    low = (rest - mid.astype(F32)).astype(BF16)
    return high, mid, low


def kernel(sizes, q_hbm, batch_ref, out_hbm, in_hbm, train_ref, scale_hbm, res_ref,
           q_ref, out_ref_in, in_ref_in, scale_ref,
           tcat, preb, right, left, scale_x, part, got,
           l_sem, t_sem, z_send, z_recv, y_send, y_recv, m_send, m_recv):
    dp, nmod, own_q, mods, width, tiles, rows_t = sizes
    half_q = own_q // 2
    group = 16
    kts = group // mods
    cuts = tiles // kts
    rows = tiles * mods
    cols = own_q * group
    y, z, md = lax.axis_index("grp"), lax.axis_index("dp"), lax.axis_index("mod")
    other = 1 - y

    locals_in = [
        pltpu.make_async_copy(src, dst, l_sem.at[i])
        for i, (src, dst) in enumerate(
            ((out_hbm, out_ref_in), (in_hbm, in_ref_in), (q_hbm, q_ref), (scale_hbm, scale_ref)))
    ]
    for copy in locals_in:
        copy.start()

    barrier = pltpu.get_barrier_semaphore()
    pl.semaphore_signal(barrier, inc=1, device_id={"grp": other}, device_id_type=MESH)

    @pl.when(z > 0)
    def _():
        pl.semaphore_signal(barrier, inc=1, device_id={"dp": z - 1}, device_id_type=MESH)

    @pl.when(z < dp - 1)
    def _():
        pl.semaphore_signal(barrier, inc=1, device_id={"dp": z + 1}, device_id_type=MESH)

    for s in range(1, nmod):
        pl.semaphore_signal(barrier, inc=1, device_id={"mod": lax.rem(md + s, nmod)}, device_id_type=MESH)

    def train_copy(g):
        return pltpu.make_async_copy(
            train_ref.at[:, pl.ds(group * g, group), :],
            tcat.at[:, :, pl.ds(LANES * g, LANES)],
            t_sem.at[g],
        )

    for g in range(cuts):
        train_copy(g).start()

    spread = ones_where(iota((width, 4 * width), 0) == iota((width, 4 * width), 1) % width)
    shape4 = (mods, 2, width, 4 * width)
    block = iota(shape4, 3) // width
    keep_r = (block % 2) == ((block // 2) ^ iota(shape4, 1))
    line = iota((2 * rows, mods * width), 0)
    line_half, line_in = line // rows, line % rows
    src = iota((2 * rows, mods * width), 1)
    pick_rows = ones_where((src // width == line_in % mods) & (src % width == 2 * (line_in // mods) + line_half))
    lcol = iota((width, 2 * rows), 1)
    col_half, col_in = lcol // rows, lcol % rows
    pick_cols = [
        ones_where(iota((width, 2 * rows), 0) == 2 * (col_in // mods) + (col_half ^ h)) for h in range(2)
    ]
    keep_l = iota((rows, 2 * rows), 0) % mods == iota((rows, 2 * rows), 1) % mods
    locals_in[0].wait()
    locals_in[1].wait()
    for b in range(2):
        for i, piece in enumerate(pieces(in_ref_in[b].reshape(mods * width, width))):
            wide = mat(piece, spread).reshape(mods, 1, width, 4 * width)
            wide = jnp.where(keep_r, jnp.broadcast_to(wide, shape4), 0.0)
            right[b, i] = wide.reshape(mods * 2 * width, 4 * width).astype(BF16)
        for i, piece in enumerate(pieces(out_ref_in[b].reshape(mods * width, width))):
            lines = mat(pick_rows, piece).astype(BF16)
            for h in range(2):
                full = mat(lines[h * rows:(h + 1) * rows], pick_cols[h])
                left[b, i, h * rows:(h + 1) * rows] = jnp.where(keep_l, full, 0.0).astype(BF16)

    def precondition(q, slot, at):
        b = batch_ref[q]
        x = q_ref[q]
        row_mod = iota((rows, LANES), 0) % mods
        zero = jnp.zeros_like(x)
        wide = jnp.concatenate([jnp.where(row_mod == m, x, zero) for m in range(mods)], axis=1)
        pair = mat(wide, right[b, 0]) + mat(wide, right[b, 1])
        stacked = jnp.concatenate([pair[:, :LANES], pair[:, LANES:]], axis=0)
        high, low = pieces(stacked)
        both = mat(left[b, 0], high) + (mat(left[b, 0], low) + mat(left[b, 1], high))
        lane = iota((rows, LANES), 1)
        pre = jnp.where(lane < width, both[:rows], both[rows:]).astype(BF16)
        for g in range(cuts):
            preb[z, slot, at, :, g * LANES:(g + 1) * LANES] = pre[g * group:(g + 1) * group]

    def z_copy(origin, i, way):
        return pltpu.make_async_remote_copy(
            src_ref=preb.at[origin, y, i], dst_ref=preb.at[origin, y, i],
            send_sem=z_send.at[way, origin, i], recv_sem=z_recv.at[origin, i],
            device_id={"dp": z + (1 - 2 * way)}, device_id_type=MESH)

    def y_copy(origin, part_at, i):
        return pltpu.make_async_remote_copy(
            src_ref=preb.at[origin, part_at, i], dst_ref=preb.at[origin, part_at, i],
            send_sem=y_send.at[origin, i], recv_sem=y_recv.at[origin, i],
            device_id={"grp": other}, device_id_type=MESH)

    def m_copy(to, frm):
        return pltpu.make_async_remote_copy(
            src_ref=part.at[to], dst_ref=got.at[frm],
            send_sem=m_send.at[to], recv_sem=m_recv.at[frm],
            device_id={"mod": to}, device_id_type=MESH)

    def has_next(way):
        return z < dp - 1 if way == 0 else z > 0

    locals_in[2].wait()
    for i in range(half_q):
        precondition(y * half_q + i, y, i)
        if i == 0:
            at_end = (z == 0) | (z == dp - 1)

            @pl.when(at_end)
            def _():
                pl.semaphore_wait(barrier, nmod + 1)

            @pl.when(jnp.logical_not(at_end))
            def _():
                pl.semaphore_wait(barrier, nmod + 2)

        for way in range(2):
            @pl.when(has_next(way))
            def _():
                z_copy(z, i, way).start()

    def score(origin):
        pre = preb[origin].reshape(cols, cuts * LANES)
        raw = mat_t(tcat[...].reshape(rows_t * group, cuts * LANES), pre).reshape(rows_t, group, cols)
        keep = iota((rows_t, group, cols), 1) == iota((rows_t, group, cols), 2) % group
        picked = jnp.sum(jnp.where(keep, raw, 0.0), axis=1) * scale_x[...]
        part[origin] = sum(mat_t(fold, p) for p in three(picked))

        @pl.when(origin != md)
        def _():
            m_copy(origin, md).start()

    def source(d, way):
        origin = z - d if way == 0 else z + d
        return jnp.clip(origin, 0, dp - 1), (origin >= 0) & (origin < dp)

    def pass_on(d, i):
        for way in range(2):
            origin, there = source(d, way)

            @pl.when(there)
            def _():
                z_copy(origin, i, way).wait_recv()

                @pl.when(has_next(way))
                def _():
                    z_copy(origin, i, way).start()

                y_copy(origin, y, i).start()

    def use(d):
        for way in range(2):
            origin, there = source(d, way)

            @pl.when(there)
            def _():
                for i in range(half_q):
                    y_copy(origin, other, i).wait_recv()
                score(origin)

    for i in range(half_q):
        pass_on(1, i)
        precondition(other * half_q + i, other, i)

    locals_in[3].wait()
    pick_mod = ones_where(iota((mods, cols), 0) == iota((mods, cols), 1) % mods)
    scale_x[...] = sum(
        lax.dot_general(p, pick_mod, (((0,), (0,)), ((), ())), preferred_element_type=F32)
        for p in three(scale_ref[...]))
    fold = ones_where(iota((own_q, cols), 1) // group == iota((own_q, cols), 0))

    for g in range(cuts):
        train_copy(g).wait()

    score(z)

    def step(d, carry):
        for i in range(half_q):
            pass_on(d, i)
        use(d - 1)
        return carry

    lax.fori_loop(2, dp, step, 0)
    use(dp - 1)

    total = part[md]
    for s in range(1, nmod):
        frm = lax.rem(md + s, nmod)
        m_copy(md, frm).wait_recv()
        total = total + got[frm]
    res_ref[...] = total

    def drain(origin, carry):
        for i in range(half_q):
            @pl.when((origin <= z) & (z < dp - 1))
            def _():
                z_copy(origin, i, 0).wait_send()

            @pl.when((origin >= z) & (z > 0))
            def _():
                z_copy(origin, i, 1).wait_send()

            @pl.when(origin != z)
            def _():
                y_copy(origin, y, i).wait_send()

        return carry

    lax.fori_loop(0, dp, drain, 0)
    for s in range(1, nmod):
        m_copy(lax.rem(md + s, nmod), md).wait_send()


def shards(queries, batch, inv_out, inv_in, train_store, row_scale):
    own_q, mods, flat = queries.shape
    width = inv_in.shape[-1]
    rows_t = train_store.shape[0]
    dp, nmod = lax.axis_size("dp"), lax.axis_size("mod")
    tiles = flat // LANES
    rows = tiles * mods

    def by_tile(a):
        return jnp.transpose(a.reshape(-1, mods, tiles, LANES), (0, 2, 1, 3)).reshape(-1, rows, LANES)

    sizes = (dp, nmod, own_q, mods, width, tiles, rows_t)
    vmem = pl.BlockSpec(memory_space=pltpu.VMEM)
    hbm = pl.BlockSpec(memory_space=pl.ANY)
    half_q = own_q // 2
    cuts = rows // 16
    return pl.pallas_call(
        functools.partial(kernel, sizes),
        out_shape=jax.ShapeDtypeStruct((own_q, rows_t), F32),
        in_specs=[hbm, pl.BlockSpec(memory_space=pltpu.SMEM), hbm, hbm, hbm, hbm],
        out_specs=vmem,
        scratch_shapes=[
            pltpu.VMEM((own_q, rows, LANES), BF16),
            pltpu.VMEM(inv_out.shape, F32),
            pltpu.VMEM(inv_in.shape, F32),
            pltpu.VMEM((mods, rows_t), F32),
            pltpu.VMEM((rows_t, 16, cuts * LANES), BF16),
            pltpu.VMEM((dp, 2, own_q // 2, 16, cuts * LANES), BF16),
            pltpu.VMEM((2, 2, mods * 2 * width, 4 * width), BF16),
            pltpu.VMEM((2, 2, 2 * rows, 2 * rows), BF16),
            pltpu.VMEM((rows_t, own_q * 16), F32),
            pltpu.VMEM((nmod, own_q, rows_t), F32),
            pltpu.VMEM((nmod, own_q, rows_t), F32),
            pltpu.SemaphoreType.DMA((4,)),
            pltpu.SemaphoreType.DMA((cuts,)),
            pltpu.SemaphoreType.DMA((2, dp, half_q)),
            pltpu.SemaphoreType.DMA((dp, half_q)),
            pltpu.SemaphoreType.DMA((dp, half_q)),
            pltpu.SemaphoreType.DMA((dp, half_q)),
            pltpu.SemaphoreType.DMA((nmod,)),
            pltpu.SemaphoreType.DMA((nmod,)),
        ],
        compiler_params=pltpu.CompilerParams(
            collective_id=0, has_side_effects=True, vmem_limit_bytes=60 * 1024 * 1024),
    )(by_tile(queries), batch, inv_out, inv_in, by_tile(train_store), jnp.transpose(row_scale))


def solution(mesh):
    in_specs = (
        P("dp", "mod", None),
        P("dp"),
        P(None, "mod", None, None),
        P(None, "mod", None, None),
        P(("grp", "dp"), "mod", None),
        P(("grp", "dp"), "mod"),
    )
    out_specs = P("mod", ("grp", "dp"))
    return jax.shard_map(shards, mesh=mesh, in_specs=in_specs, out_specs=out_specs, check_vma=False)
```
